32 devices in a mesh: seq: 16 (over z, y, x), tp: 2 (over core).
Axes of the slice: x: 2, y: 2, z: 4, core: 2. Of those that a mesh axis runs over, the one named last changes fastest.
Arguments:
- queries: bfloat16 [1024, 8192], P('seq', 'tp'), may hold values from -8 to 8
- keys: bfloat16 [1024, 1024], P('seq', 'tp'), may hold values from -8 to 8
- values: bfloat16 [1024, 1024], P('seq', 'tp'), may hold values from -6 to 6
- segment_ids: int32 [1024], P('seq'), may hold values from 0 to 5, as said below
- out_weight: bfloat16 [8192, 16384], P('tp', 'seq'), may hold values from -0.0625 to 0.0625
Outputs:
- mixed: bfloat16 [1024, 16384], P('tp', 'seq')
The draws below stay inside these ranges and needn't reach their ends.
Inputs may be any that keep to these rules, and one draw needn't show every extreme that they name: `segment_ids`: document ids start at 0 at the first token, never fall, and rise by at most one from a token to the next; one document covers exactly 576 tokens.
All inputs are finite; a program needn't handle non-finite values.
Results may differ from the reference program's by a relative error of at most 0.019.
Values may be sent and summed in bfloat16 or wider, within the bound.
A program may use at most 64 MiB of HBM per device.

```python
import math
import jax
import jax.numpy as jnp
from jax import lax

TOK_DEV = 64
HD = 128
KVH = 8
GROUP = 8
D = 16384
TOKENS = 1024


def doc_segments(key):
    key = jax.random.fold_in(key, 11)
    order_key, begin_key = jax.random.split(key)
    token_index = jnp.arange(TOKENS, dtype=jnp.int32)
    long_length = TOKENS // 2 + TOK_DEV
    long_start = jax.random.randint(begin_key, (), 1, TOKENS - long_length)
    long_end = long_start + long_length
    extra_count = max(1, (TOKENS // 2 - TOK_DEV) // 128)
    ranking = jax.random.permutation(order_key, TOKENS).astype(jnp.int32)
    blocked = (token_index >= long_start) & (token_index <= long_end) | (token_index == 0)
    ranking = jnp.where(blocked, -1, ranking)
    picked_values, picked_index = lax.top_k(ranking, extra_count)
    extra_flags = jnp.zeros((TOKENS,), jnp.int32).at[picked_index].set(1)
    start_flags = (extra_flags == 1) | (token_index == long_start) | (token_index == long_end) | (token_index == 0)
    return jnp.cumsum(start_flags.astype(jnp.int32)) - 1


def draw_segment_ids(key, part):
    return doc_segments(key)


def draw_queries(key, part):
    key = jax.random.fold_in(key, 3)
    full_shape = (TOKENS, KVH, GROUP, HD)
    base_draw = jnp.clip(jax.random.normal(key, full_shape), -6.0, 6.0)
    return base_draw.reshape(TOKENS, KVH * GROUP * HD).astype(jnp.bfloat16)


def draw_keys(key, part):
    key = jax.random.fold_in(key, 5)
    full_shape = (TOKENS, KVH, HD)
    base_draw = jnp.clip(jax.random.normal(key, full_shape), -6.0, 6.0)
    return base_draw.reshape(TOKENS, KVH * HD).astype(jnp.bfloat16)


def level_of(stream_key, shape, shards, smallest, largest):
    gain = 1.0
    for axis_at, shards_of in shards:
        heights = jax.random.uniform(jax.random.fold_in(jax.random.fold_in(stream_key, 6), axis_at), (shards_of,), jnp.float32, smallest / len(shards), largest / len(shards))
        gain = gain * jnp.repeat(jnp.exp(heights), shape[axis_at] // shards_of).reshape((-1,) + (1,) * (len(shape) - 1 - axis_at))
    return gain


def bell_draw(stream_key, dims, spread, most, cuts=(), held_as=jnp.bfloat16):
    factor_of = level_of(stream_key, dims, cuts, -0.22, 0.18) if cuts else 1.0
    values = jax.random.normal(stream_key, dims, jnp.float32) * spread * factor_of
    return jnp.minimum(jnp.maximum(values, -most), most).astype(held_as)


def setup_inputs(seed: int = 0) -> dict:
    arg_keys = jax.random.split(jax.random.key(seed), 6)
    queries = draw_queries(jax.random.fold_in(arg_keys[5], 71), 0)
    keys = draw_keys(jax.random.fold_in(arg_keys[5], 71), 0)
    values = bell_draw(arg_keys[2], (TOKENS, KVH * HD), 1.0, 6.0, ((0, 16), (1, 2)))
    segment_ids = draw_segment_ids(jax.random.fold_in(arg_keys[5], 71), 0)
    out_weight = bell_draw(arg_keys[4], (KVH * GROUP * HD, D), (KVH * GROUP * HD) ** -0.5, 0.0625, ((0, 2), (1, 16)))
    return dict(queries=queries, keys=keys, values=values, segment_ids=segment_ids, out_weight=out_weight)


masked_score = -1e+30

def reference(queries, keys, values, segment_ids, out_weight):
    score_scale = 1.0 / math.sqrt(HD)
    query_heads = queries.reshape(TOKENS, KVH, GROUP, HD).astype(jnp.float32)
    key_heads = keys.reshape(TOKENS, KVH, HD).astype(jnp.float32)
    value_heads = values.reshape(TOKENS, KVH, HD).astype(jnp.float32)
    key_pos = jnp.arange(TOKENS, dtype=jnp.int32)

    def query_block(first_row):
        block_rows = lax.dynamic_slice_in_dim(query_heads, first_row, TOK_DEV, 0)
        query_pos = first_row + jnp.arange(TOK_DEV, dtype=jnp.int32)
        query_seg = lax.dynamic_slice_in_dim(segment_ids, first_row, TOK_DEV, 0)
        allowed = (key_pos[None, :] <= query_pos[:, None]) & (segment_ids[None, :] == query_seg[:, None])
        keep_mask = allowed[:, None, None, :]
        scores = jnp.einsum('tkgd,skd->tkgs', block_rows, key_heads, precision=lax.Precision.HIGHEST) * score_scale
        row_max = lax.optimization_barrier(jnp.max(jnp.where(keep_mask, scores, masked_score), axis=-1))
        weights = jnp.where(keep_mask, jnp.exp(scores - row_max[..., None]), 0.0)
        row_sum = lax.optimization_barrier(jnp.sum(weights, axis=-1))
        rounded = lax.optimization_barrier(weights.astype(jnp.bfloat16)).astype(jnp.float32)
        combined = jnp.einsum('tkgs,skd->tkgd', rounded, value_heads, precision=lax.Precision.HIGHEST)
        return (combined / row_sum[..., None]).astype(jnp.bfloat16).reshape(TOK_DEV, KVH * GROUP * HD)
    starts = jnp.arange(TOKENS // TOK_DEV, dtype=jnp.int32) * TOK_DEV
    attended = lax.map(query_block, starts).reshape(TOKENS, KVH * GROUP * HD)
    return jnp.dot(attended, out_weight, preferred_element_type=jnp.float32).astype(jnp.bfloat16)
```

```python
import functools
import math

import jax
import jax.numpy as jnp
from jax import lax
from jax.experimental import pallas as pl
from jax.experimental.pallas import tpu as pltpu
from jax.sharding import PartitionSpec as P

HD = 128
GROUP = 8
MESH = pl.DeviceIdType.MESH

masked_score = -1e30


def body(queries, keys, values, segment_ids, out_weight):
    seq_rank = lax.axis_index("seq")
    tok_count = queries.shape[0]
    local_heads = keys.shape[1] // HD
    score_scale = 1.0 / math.sqrt(HD)
    all_segments = lax.all_gather(segment_ids, "seq", axis=0, tiled=True)
    offsets = jnp.arange(tok_count, dtype=jnp.int32)
    positions = seq_rank * tok_count + offsets
    query_segments = jnp.take(all_segments, positions)
    grouped = queries.reshape(tok_count, local_heads, GROUP, HD)
    key_block = lax.all_gather(keys, "seq", axis=0, tiled=True)
    value_block = lax.all_gather(values, "seq", axis=0, tiled=True)
    block_rows = key_block.shape[0]
    key_pos = jnp.arange(block_rows, dtype=jnp.int32)
    allowed = (key_pos[None, :] <= positions[:, None]) & (
        all_segments[None, :] == query_segments[:, None]
    )
    running_max = jnp.full((local_heads, tok_count, GROUP), masked_score, jnp.float32)
    key_heads = key_block.reshape(block_rows, local_heads, HD)
    value_heads = value_block.reshape(block_rows, local_heads, HD)
    scores = (
        jnp.einsum("thgd,nhd->htgn", grouped, key_heads, preferred_element_type=jnp.float32)
        * score_scale
    )
    keep_mask = allowed[None, :, None, :]
    new_max = jnp.maximum(running_max, jnp.max(jnp.where(keep_mask, scores, masked_score), axis=-1))
    weights = jnp.where(keep_mask, jnp.exp(scores - new_max[..., None]), 0.0)
    running_sum = jnp.sum(weights, axis=-1)
    summed = jnp.einsum(
        "htgn,nhd->htgd",
        weights.astype(jnp.bfloat16),
        value_heads,
        preferred_element_type=jnp.float32,
    )
    attended = (
        (summed / running_sum[..., None])
        .transpose(1, 0, 2, 3)
        .reshape(tok_count, local_heads * GROUP * HD)
    )
    attended = attended.astype(jnp.bfloat16)
    partial_out = jnp.dot(
        lax.all_gather(attended, "seq", axis=0, tiled=True),
        out_weight,
        preferred_element_type=jnp.float32,
    )
    summed_out = lax.psum_scatter(
        partial_out.astype(jnp.bfloat16), "tp", scatter_dimension=0, tiled=True
    )
    return summed_out


NZ = 4
TOK = 64
LAYER = 4 * TOK
TOKENS = NZ * LAYER
HEADS = 4
WIDE = GROUP * HD

ROUTES = ("a", "b", "l", "a")

ORDER = (
    [("kv", 0), ("kv", 1)]
    + [("kvz", 0, t) for t in (1, 2, 3)]
    + [("kvn1", 0, t) for t in range(4)]
    + [("kvn2", 0, t) for t in range(4)]
    + [("kvz", 1, t) for t in (1, 2, 3)]
    + [("mask",), ("attn", 0)]
    + [("kvn1", 1, t) for t in range(4)]
    + [("z", 0, 1)]
    + [("kvn2", 1, t) for t in range(4)]
    + [("attn", 1)]
    + [("n1", 0, 0), ("z", 0, 2), ("z", 1, 1)]
    + [("attn", 2)]
    + [("z", 0, 3), ("n1", 0, 1), ("n1", 1, 0), ("z", 1, 2), ("l1", 2)]
    + [("attn", 3)]
    + [("z", 1, 3), ("z", 3, 1), ("l2", 2, 0), ("n1", 0, 2), ("n1", 1, 1), ("n1", 3, 0), ("l2", 2, 1)]
    + [("mm", 0, 0), ("z", 3, 2), ("n1", 0, 3), ("n1", 1, 2), ("z", 3, 3), ("mm", 1, 0)]
    + [("lz", 2, 1, 0), ("n1", 1, 3), ("n1", 3, 1), ("mm", 0, 1), ("lz", 2, 1, 1), ("n1", 3, 2)]
    + [("lz", 2, 1, 2), ("n1", 3, 3), ("mm", 1, 1), ("lz", 2, 1, 3), ("mm", 3, 0), ("ml", 2, 0)]
    + [("mm", 3, 1), ("ml", 2, 1)]
    + [("n2", 0), ("mm", 0, 2), ("mm", 0, 3)]
    + [("lz", 2, 2, w) for w in range(4)]
    + [("n2", 1), ("mm", 1, 2), ("mm", 1, 3), ("ml", 2, 2)]
    + [("lz", 2, 3, w) for w in range(4)]
    + [("ml", 2, 3), ("n2", 3), ("mm", 3, 2), ("mm", 3, 3)]
)


def block_kernel(q_ref, k_ref, v_ref, seg_ref, w_hbm, out_ref,
                 kv0, kv1, att, wt, acc, bias, outgoing, incoming,
                 w_sem, send_sems, kv_sems, z_sems, p_sems, l_sems, tp_sems):
    me = lax.axis_index("seq")
    core = lax.axis_index("tp")
    z = me // 4
    w = me % 4
    x = w % 2
    y = w // 2
    w_x = y * 2 + (1 - x)
    w_y = (1 - y) * 2 + x
    w_d = (1 - y) * 2 + (1 - x)
    w_a = jnp.where(core == 0, w_x, w_y)
    w_b = jnp.where(core == 0, w_y, w_x)
    planes = {"a": (w_a, w_b), "b": (w_b, w_a), "l": (w_a, w_b)}

    def nearest(t):
        table = ((0, 1, 2, 3), (1, 0, 2, 3), (2, 3, 1, 0), (3, 2, 1, 0))
        at = jnp.int32(table[0][t])
        for layer in range(1, NZ):
            at = jnp.where(z == layer, table[layer][t], at)
        return at

    layers = [z if t == 0 else nearest(t) for t in range(NZ)]
    has_up = z < NZ - 1
    has_down = z > 0
    sends = []

    def at_rows(layer, column):
        return pl.ds(pl.multiple_of(layer * LAYER + column * TOK, TOK), TOK)

    def copy_of(ref, recv_sem, device, send_sem):
        return pltpu.make_async_remote_copy(
            src_ref=ref, dst_ref=ref, send_sem=send_sem, recv_sem=recv_sem,
            device_id=(device, core), device_id_type=MESH)

    def send(ref, recv_sem, device, guard=None):
        copy = copy_of(ref, recv_sem, device, send_sems.at[len(sends)])
        sends.append((copy, guard))
        if guard is None:
            copy.start()
        else:
            pl.when(guard)(copy.start)

    def arrive(ref, recv_sem, guard=None):
        copy = copy_of(ref, recv_sem, me, send_sems.at[0])
        if guard is None:
            copy.wait_recv()
        else:
            pl.when(guard)(copy.wait_recv)

    kvs = (kv0, kv1)

    def kv_route(g):
        return planes["a"] if g == 0 else planes["b"]

    def kv_out(g, t, guard):
        n1, n2 = kv_route(g)
        ref = kvs[g].at[at_rows(z - t, w)]
        if t < NZ - 1:
            up = has_up if guard is None else jnp.logical_and(guard, has_up)
            send(ref, kv_sems.at[g, t + 1], me + 4, up)
        send(ref, kv_sems.at[g, 4 + t], z * 4 + n1, guard)
        send(ref, kv_sems.at[g, 8 + t], z * 4 + n2, guard)

    def kv_own(g):
        kv_out(g, 0, None)

    def kv_z(g, t):
        guard = z >= t
        arrive(kvs[g].at[at_rows(z - t, w)], kv_sems.at[g, t], guard)
        kv_out(g, t, guard)

    def kv_n1(g, t):
        n1, n2 = kv_route(g)
        guard = None if t == 0 else z >= t
        ref = kvs[g].at[at_rows(z - t, n1)]
        arrive(ref, kv_sems.at[g, 4 + t], guard)
        send(ref, kv_sems.at[g, 12 + t], z * 4 + n2, guard)

    def kv_n2(g, t):
        n1, n2 = kv_route(g)
        guard = None if t == 0 else z >= t
        arrive(kvs[g].at[at_rows(z - t, n2)], kv_sems.at[g, 8 + t], guard)
        arrive(kvs[g].at[at_rows(z - t, w_d)], kv_sems.at[g, 12 + t], guard)

    def make_mask():
        ones = jnp.full((8, HD), 1.0 / HD, jnp.bfloat16)
        key_segments = lax.dot_general(
            ones, kv0[:, 2 * HD:3 * HD], (((1,), (1,)), ((), ())),
            preferred_element_type=jnp.float32)[0:1, :]
        query_segments = seg_ref[:, 0:1].astype(jnp.float32)
        key_at = lax.broadcasted_iota(jnp.int32, (TOK, TOKENS), 1)
        query_at = me * TOK + lax.broadcasted_iota(jnp.int32, (TOK, TOKENS), 0)
        allowed = (key_at <= query_at) & (key_segments == query_segments)
        bias[...] = jnp.where(allowed, 0.0, masked_score)

    def piece(p, layer, column):
        return att.at[at_rows(layer, column), pl.ds(p * WIDE, WIDE)]

    def z_sem(p, layer, column):
        return z_sems.at[p, layer]

    def l_sem(p, layer, c):
        return l_sems.at[4 + c * 4 + layer]

    def out_along_z(p, ref, sem):
        send(ref, sem, me + 4, has_up)
        send(ref, sem, me - 4, has_down)

    def on_along_z(ref, sem, layer):
        upward = layer < z
        further = jnp.where(upward, has_up, has_down)
        send(ref, sem, jnp.where(upward, me + 4, me - 4), further)

    def attend(p):
        kv, at, count = (kv0, 0, 1) if p == 0 else (kv1, p - 1, HEADS - 1)
        k_cols = pl.ds(at * HD, HD)
        v_cols = pl.ds((count + at) * HD, HD)
        half = GROUP // 2

        def heads(i, carry):
            column = pl.multiple_of(p * WIDE + i * half * HD, HD)
            rows = jnp.concatenate(
                [q_ref[:, pl.ds(pl.multiple_of(column + g * HD, HD), HD)] for g in range(half)], axis=0)
            scores = lax.dot_general(
                rows, kv[:, k_cols], (((1,), (1,)), ((), ())),
                preferred_element_type=jnp.float32) * (1.0 / math.sqrt(HD))
            scores = scores.reshape(half, TOK, TOKENS) + bias[...][None]
            weights = jnp.exp(scores - jnp.max(scores, axis=-1, keepdims=True))
            total = jnp.sum(weights, axis=-1, keepdims=True)
            summed = jnp.dot(
                weights.reshape(half * TOK, TOKENS).astype(jnp.bfloat16), kv[:, v_cols],
                preferred_element_type=jnp.float32)
            done = (summed.reshape(half, TOK, HD) / total).astype(jnp.bfloat16)
            for g in range(half):
                att[at_rows(z, w), pl.ds(pl.multiple_of(column + g * HD, HD), HD)] = done[g]
            return carry

        lax.fori_loop(0, 2, heads, 0)
        ref = piece(p, z, w)
        n1, n2 = planes[ROUTES[p]]
        if ROUTES[p] == "l":
            send(ref, l_sems.at[0], z * 4 + n1)
            send(ref, l_sems.at[1], z * 4 + n2)
            out_along_z(p, ref, l_sem(p, z, 0))
        else:
            out_along_z(p, ref, z_sem(p, z, 0))
            send(ref, p_sems.at[p, 0], z * 4 + n1)
            send(ref, p_sems.at[p, 4], z * 4 + n2)

    def from_z(p, t):
        n1, n2 = planes[ROUTES[p]]
        ref = piece(p, layers[t], w)
        sem = z_sem(p, layers[t], 0)
        arrive(ref, sem)
        on_along_z(ref, sem, layers[t])
        send(ref, p_sems.at[p, t], z * 4 + n1)
        send(ref, p_sems.at[p, 4 + t], z * 4 + n2)

    def from_n1(p, t):
        n1, n2 = planes[ROUTES[p]]
        ref = piece(p, layers[t], n1)
        arrive(ref, p_sems.at[p, t])
        send(ref, p_sems.at[p, 8 + t], z * 4 + n2)

    def from_n2(p):
        n1, n2 = planes[ROUTES[p]]
        for t in range(NZ):
            arrive(piece(p, layers[t], n2), p_sems.at[p, 4 + t])
            arrive(piece(p, layers[t], w_d), p_sems.at[p, 8 + t])

    def columns_of(p):
        n1, n2 = planes[ROUTES[p]]
        return (w, n1, n2, w_d)

    def l_from_n1(p):
        n1, n2 = planes[ROUTES[p]]
        ref = piece(p, z, n1)
        arrive(ref, l_sems.at[0])
        send(ref, l_sems.at[2], z * 4 + n2)
        out_along_z(p, ref, l_sem(p, z, 1))

    def l_from_n2(p, c):
        ref = piece(p, z, columns_of(p)[2 + c])
        arrive(ref, l_sems.at[1 + c])
        out_along_z(p, ref, l_sem(p, z, 2 + c))

    def l_from_z(p, t, c):
        ref = piece(p, layers[t], columns_of(p)[c])
        sem = l_sem(p, layers[t], c)
        arrive(ref, sem)
        on_along_z(ref, sem, layers[t])

    waited = []

    def project(p, rows):
        if not waited:
            waited.append(True)
            pltpu.make_async_copy(w_hbm, wt, w_sem).wait()
        left = jnp.concatenate([att[r, pl.ds(p * WIDE, WIDE)] for r in rows], axis=0)

        def tile(n, carry):
            cols = pl.ds(pl.multiple_of(n * 256, 256), 256)
            part = jnp.dot(left, wt[pl.ds(p * WIDE, WIDE), cols], preferred_element_type=jnp.float32)
            for i, r in enumerate(rows):
                acc[r, cols] += part[i * TOK:(i + 1) * TOK]
            return carry

        lax.fori_loop(0, acc.shape[1] // 256, tile, 0)

    def project_column(p, c):
        project(p, [at_rows(layer, columns_of(p)[c]) for layer in range(NZ)])

    def project_layer(p, t):
        project(p, [at_rows(layers[t], c) for c in range(4)])

    pltpu.make_async_copy(w_hbm, wt, w_sem).start()
    kv0[...] = jnp.zeros_like(kv0)
    kv1[...] = jnp.zeros_like(kv1)
    own = at_rows(z, w)
    kv0[own, 0:HD] = k_ref[:, 0:HD]
    kv0[own, HD:2 * HD] = v_ref[:, 0:HD]
    kv0[own, 2 * HD:3 * HD] = seg_ref[...]
    kv1[own, 0:3 * HD] = k_ref[:, HD:]
    kv1[own, 3 * HD:6 * HD] = v_ref[:, HD:]

    barrier = pltpu.get_barrier_semaphore()

    def greet(device, at_core):
        pl.semaphore_signal(barrier, inc=1, device_id=(device, at_core), device_id_type=MESH)

    greet(me, 1 - core)
    greet(z * 4 + w_x, core)
    greet(z * 4 + w_y, core)
    pl.when(has_up)(lambda: greet(me + 4, core))
    pl.when(has_down)(lambda: greet(me - 4, core))
    acc[...] = jnp.zeros_like(acc)
    inner = jnp.logical_and(has_up, has_down)
    pl.semaphore_wait(barrier, jnp.where(inner, 5, 4))

    steps = {"kv": kv_own, "kvz": kv_z, "kvn1": kv_n1, "kvn2": kv_n2, "mask": make_mask,
             "attn": attend, "z": from_z, "n1": from_n1, "n2": from_n2,
             "l1": l_from_n1, "l2": l_from_n2, "lz": l_from_z,
             "mm": project_column, "ml": project_layer}
    for step in ORDER:
        steps[step[0]](*step[1:])

    half = TOKENS // 2
    chunk = half // 4
    copies = []
    for i in range(4):
        rows = pl.ds(i * chunk, chunk)
        theirs = pl.ds(pl.multiple_of((1 - core) * half + i * chunk, chunk), chunk)
        outgoing[rows, :] = acc[theirs, :].astype(jnp.bfloat16)
        copy = pltpu.make_async_remote_copy(
            src_ref=outgoing.at[rows], dst_ref=incoming.at[rows],
            send_sem=tp_sems.at[i], recv_sem=tp_sems.at[4 + i],
            device_id=(me, 1 - core), device_id_type=MESH)
        copy.start()
        copies.append(copy)
    for copy, guard in sends:
        if guard is None:
            copy.wait_send()
        else:
            pl.when(guard)(copy.wait_send)
    for i in range(4):
        rows = pl.ds(i * chunk, chunk)
        ours = pl.ds(pl.multiple_of(core * half + i * chunk, chunk), chunk)
        copies[i].wait()
        out_ref[rows, :] = (acc[ours, :] + incoming[rows, :].astype(jnp.float32)).astype(jnp.bfloat16)


def count_sends():
    each = {"kv": 3, "kvz": 3, "kvn1": 1, "z": 3, "n1": 1, "l1": 3, "l2": 2, "lz": 1, "attn": 4}
    return sum(each.get(step[0], 0) for step in ORDER)


def kernel_body(queries, keys, values, segment_ids, out_weight):
    segments = jnp.broadcast_to(segment_ids.astype(jnp.bfloat16)[:, None], (TOK, HD))
    width = out_weight.shape[1]
    vmem = pl.BlockSpec(memory_space=pltpu.VMEM)
    dma = pltpu.SemaphoreType.DMA
    return pl.pallas_call(
        block_kernel,
        out_shape=jax.ShapeDtypeStruct((TOKENS // 2, width), jnp.bfloat16),
        in_specs=[vmem, vmem, vmem, vmem, pl.BlockSpec(memory_space=pl.ANY)],
        out_specs=vmem,
        scratch_shapes=[
            pltpu.VMEM((TOKENS, 3 * HD), jnp.bfloat16),
            pltpu.VMEM((TOKENS, 6 * HD), jnp.bfloat16),
            pltpu.VMEM((TOKENS, HEADS * WIDE), jnp.bfloat16),
            pltpu.VMEM((HEADS * WIDE, width), jnp.bfloat16),
            pltpu.VMEM((TOKENS, width), jnp.float32),
            pltpu.VMEM((TOK, TOKENS), jnp.float32),
            pltpu.VMEM((TOKENS // 2, width), jnp.bfloat16),
            pltpu.VMEM((TOKENS // 2, width), jnp.bfloat16),
            dma,
            dma((count_sends(),)),
            dma((2, 16)),
            dma((HEADS, NZ)),
            dma((HEADS, 12)),
            dma((20,)),
            dma((8,)),
        ],
        compiler_params=pltpu.CompilerParams(
            collective_id=0, has_side_effects=True, vmem_limit_bytes=56 * 1024 * 1024),
        cost_estimate=pl.CostEstimate(
            flops=2 * TOKENS * HEADS * WIDE * width, bytes_accessed=16 * 2**20, transcendentals=2**21),
    )(queries, keys, values, segments, out_weight)


def solution(mesh):
    fits = mesh.shape["seq"] == 4 * NZ and mesh.shape["tp"] == 2
    return jax.shard_map(
        kernel_body if fits else body,
        mesh=mesh,
        in_specs=(P("seq", "tp"), P("seq", "tp"), P("seq", "tp"), P("seq"), P("tp", "seq")),
        out_specs=P("tp", "seq"),
        check_vma=False,
    )
```

```python
import functools
import math

import jax
import jax.numpy as jnp
from jax import lax
from jax.experimental import pallas as pl
from jax.experimental.pallas import tpu as pltpu
from jax.sharding import PartitionSpec as P

HD = 128
GROUP = 8
MESH = pl.DeviceIdType.MESH

masked_score = -1e30


def body(queries, keys, values, segment_ids, out_weight):
    seq_rank = lax.axis_index("seq")
    tok_count = queries.shape[0]
    local_heads = keys.shape[1] // HD
    score_scale = 1.0 / math.sqrt(HD)
    all_segments = lax.all_gather(segment_ids, "seq", axis=0, tiled=True)
    offsets = jnp.arange(tok_count, dtype=jnp.int32)
    positions = seq_rank * tok_count + offsets
    query_segments = jnp.take(all_segments, positions)
    grouped = queries.reshape(tok_count, local_heads, GROUP, HD)
    key_block = lax.all_gather(keys, "seq", axis=0, tiled=True)
    value_block = lax.all_gather(values, "seq", axis=0, tiled=True)
    block_rows = key_block.shape[0]
    key_pos = jnp.arange(block_rows, dtype=jnp.int32)
    allowed = (key_pos[None, :] <= positions[:, None]) & (
        all_segments[None, :] == query_segments[:, None]
    )
    running_max = jnp.full((local_heads, tok_count, GROUP), masked_score, jnp.float32)
    key_heads = key_block.reshape(block_rows, local_heads, HD)
    value_heads = value_block.reshape(block_rows, local_heads, HD)
    scores = (
        jnp.einsum("thgd,nhd->htgn", grouped, key_heads, preferred_element_type=jnp.float32)
        * score_scale
    )
    keep_mask = allowed[None, :, None, :]
    new_max = jnp.maximum(running_max, jnp.max(jnp.where(keep_mask, scores, masked_score), axis=-1))
    weights = jnp.where(keep_mask, jnp.exp(scores - new_max[..., None]), 0.0)
    running_sum = jnp.sum(weights, axis=-1)
    summed = jnp.einsum(
        "htgn,nhd->htgd",
        weights.astype(jnp.bfloat16),
        value_heads,
        preferred_element_type=jnp.float32,
    )
    attended = (
        (summed / running_sum[..., None])
        .transpose(1, 0, 2, 3)
        .reshape(tok_count, local_heads * GROUP * HD)
    )
    attended = attended.astype(jnp.bfloat16)
    partial_out = jnp.dot(
        lax.all_gather(attended, "seq", axis=0, tiled=True),
        out_weight,
        preferred_element_type=jnp.float32,
    )
    summed_out = lax.psum_scatter(
        partial_out.astype(jnp.bfloat16), "tp", scatter_dimension=0, tiled=True
    )
    return summed_out


NZ = 4
TOK = 64
LAYER = 4 * TOK
TOKENS = NZ * LAYER
HEADS = 4
WIDE = GROUP * HD

ROUTES = ("a", "l", "b", "a")
KV_HEADS = ((0,), (1,), (2, 3))
KV_COLS = tuple(2 * len(heads) * HD + (HD if g == 0 else 0) for g, heads in enumerate(KV_HEADS))
KV_GROUPS = len(KV_HEADS)
KV_REACH = 9

ORDER = (
    ("kv", 0), ("kv", 1), ("kvn1", 0, 0), ("kvz", 0, 1), ("kvn1", 1, 0), ("kvz", 1, 1), ("kvz", 0, 2),
    ("kvz", 1, 2), ("kvz", 1, 3), ("kvn1", 0, 1), ("kvn1", 0, 2), ("kv", 2), ("kvz", 0, 3), ("kvn2", 0, 0),
    ("kvz", 2, 1), ("kvn1", 0, 3), ("kvn1", 1, 2), ("kvn1", 1, 1), ("kvn2", 1, 0), ("kvn2", 0, 3),
    ("kvn2", 0, 1), ("kvz", 2, 2), ("kvn2", 0, 2), ("mask",), ("kvn1", 1, 3), ("attn", 0), ("kvz", 2, 3),
    ("kvn2", 1, 1), ("kvn2", 1, 3), ("kvn2", 1, 2), ("kvn1", 2, 1), ("attn", 1), ("kvn1", 2, 0),
    ("kvn1", 2, 3), ("kvn1", 2, 2), ("kvn2", 2, 1), ("z", 0, 1), ("z", 0, 2), ("kvn2", 2, 0), ("l1", 1),
    ("kvn2", 2, 3), ("n1", 0, 0), ("kvn2", 2, 2), ("attn", 3), ("z", 0, 3), ("l2", 1, 1), ("n1", 0, 2),
    ("z", 3, 1), ("lz", 1, 1, 1), ("lz", 1, 1, 0), ("z", 3, 2), ("n1", 0, 3), ("l2", 1, 0), ("n1", 0, 1),
    ("attn", 2), ("n1", 3, 0), ("lz", 1, 2, 1), ("lz", 1, 1, 3), ("lz", 1, 2, 3), ("z", 2, 1), ("z", 3, 3),
    ("z", 2, 2), ("lz", 1, 1, 2), ("z", 2, 3), ("n1", 3, 2), ("ml", 1, 0), ("n1", 3, 1), ("mm", 0, 0),
    ("lz", 1, 3, 1), ("n2", 0, 0), ("n1", 3, 3), ("mm", 3, 1), ("n1", 2, 0), ("mm", 0, 2), ("lz", 1, 2, 0),
    ("n2", 3, 0), ("mm", 2, 0), ("mm", 0, 1), ("ml", 1, 1), ("lz", 1, 2, 2), ("n2", 2, 0), ("n2", 0, 1),
    ("ml", 1, 2), ("mm", 3, 0), ("lz", 1, 3, 3), ("n1", 2, 3), ("n1", 2, 2), ("mm", 0, 3), ("mm", 3, 2),
    ("n1", 2, 1), ("n2", 3, 1), ("mm", 2, 1), ("lz", 1, 3, 2), ("mm", 3, 3), ("mm", 2, 2), ("lz", 1, 3, 0),
    ("n2", 2, 1), ("mm", 2, 3), ("ml", 1, 3),)


def block_kernel(q_ref, k_ref, v_ref, seg_ref, w_hbm, out_ref,
                 kv0, kv1, kv2, att, wt, acc, bias, outgoing, incoming,
                 w_sem, send_sems, kv_sems, z_sems, p_sems, l_sems, share_sems, tp_sems):
    me = lax.axis_index("seq")
    core = lax.axis_index("tp")
    z = me // 4
    w = me % 4
    x = w % 2
    y = w // 2
    w_x = y * 2 + (1 - x)
    w_y = (1 - y) * 2 + x
    w_d = (1 - y) * 2 + (1 - x)
    w_a = jnp.where(core == 0, w_x, w_y)
    w_b = jnp.where(core == 0, w_y, w_x)
    planes = {"a": (w_a, w_b), "b": (w_b, w_a), "l": (w_a, w_b)}

    def nearest(t):
        table = ((0, 1, 2, 3), (1, 0, 2, 3), (2, 3, 1, 0), (3, 2, 1, 0))
        at = jnp.int32(table[0][t])
        for layer in range(1, NZ):
            at = jnp.where(z == layer, table[layer][t], at)
        return at

    layers = [z if t == 0 else nearest(t) for t in range(NZ)]
    has_up = z < NZ - 1
    has_down = z > 0
    sends = []

    def at_rows(layer, column):
        return pl.ds(pl.multiple_of(layer * LAYER + column * TOK, TOK), TOK)

    def copy_of(ref, recv_sem, device, send_sem):
        return pltpu.make_async_remote_copy(
            src_ref=ref, dst_ref=ref, send_sem=send_sem, recv_sem=recv_sem,
            device_id=(device, core), device_id_type=MESH)

    def send(ref, recv_sem, device, guard=None):
        copy = copy_of(ref, recv_sem, device, send_sems.at[len(sends)])
        sends.append((copy, guard))
        if guard is None:
            copy.start()
        else:
            pl.when(guard)(copy.start)

    def arrive(ref, recv_sem, guard=None):
        copy = copy_of(ref, recv_sem, me, send_sems.at[0])
        if guard is None:
            copy.wait_recv()
        else:
            pl.when(guard)(copy.wait_recv)

    kvs = (kv0, kv1, kv2)

    assert (NZ - 1) * 4 - KV_REACH == 3
    last = NZ - 1
    at_top = z == last

    def kv_route(g):
        return planes["a"] if g % 2 == 0 else planes["b"]

    def kv_own(g):
        kv_out(g, 0, None)

    def kv_out(g, t, guard):
        n1, n2 = kv_route(g)
        ref = kvs[g].at[at_rows(z - t, w)]
        if t < last:
            up = has_up if guard is None else jnp.logical_and(guard, has_up)
            if t == last - 1:
                up = jnp.logical_and(up, w == 3)
            send(ref, kv_sems.at[g, t + 1], me + 4, up)
        send(ref, kv_sems.at[g, 4 + t], z * 4 + n1, guard)
        if t < last:
            send(ref, kv_sems.at[g, 8 + t], z * 4 + n2, guard)

    def kv_z(g, t):
        guard = z >= t if t < last else jnp.logical_and(at_top, w == 3)
        arrive(kvs[g].at[at_rows(z - t, w)], kv_sems.at[g, t], guard)
        kv_out(g, t, guard)

    def kv_n1(g, t):
        n1, n2 = kv_route(g)
        guard = None if t == 0 else z >= t if t < last else jnp.logical_and(at_top, n1 == 3)
        ref = kvs[g].at[at_rows(z - t, n1)]
        arrive(ref, kv_sems.at[g, 4 + t], guard)
        send(ref, kv_sems.at[g, 12 + t], z * 4 + n2, guard)

    def kv_n2(g, t):
        n1, n2 = kv_route(g)
        guard = None if t == 0 else z >= t if t < last else jnp.logical_and(at_top, w == 0)
        if t < last:
            arrive(kvs[g].at[at_rows(z - t, n2)], kv_sems.at[g, 8 + t], guard)
        arrive(kvs[g].at[at_rows(z - t, w_d)], kv_sems.at[g, 12 + t], guard)

    def make_mask():
        ones = jnp.full((8, HD), 1.0 / HD, jnp.bfloat16)
        key_segments = lax.dot_general(
            ones, kv0[:, 2 * HD:3 * HD], (((1,), (1,)), ((), ())),
            preferred_element_type=jnp.float32)[0:1, :]
        query_segments = kv0[at_rows(z, w), pl.ds(2 * HD, HD)][:, 0:1].astype(jnp.float32)
        key_at = lax.broadcasted_iota(jnp.int32, (TOK, TOKENS), 1)
        query_at = me * TOK + lax.broadcasted_iota(jnp.int32, (TOK, TOKENS), 0)
        allowed = (key_at <= query_at) & (key_segments == query_segments)
        bias[...] = jnp.where(allowed, 0.0, masked_score)

    def piece(p, layer, column):
        return att.at[at_rows(layer, column), pl.ds(p * WIDE, WIDE)]

    def z_sem(p, layer, column):
        return z_sems.at[p, layer]

    def l_sem(p, layer, c):
        return l_sems.at[4 + c * 4 + layer]

    def out_along_z(p, ref, sem):
        send(ref, sem, me + 4, has_up)
        send(ref, sem, me - 4, has_down)

    def on_along_z(ref, sem, layer):
        upward = layer < z
        further = jnp.where(upward, has_up, has_down)
        send(ref, sem, jnp.where(upward, me + 4, me - 4), further)

    def attend(p):
        g = next(i for i, heads in enumerate(KV_HEADS) if p in heads)
        kv, at = kvs[g], KV_HEADS[g].index(p)
        k_cols = pl.ds(at * HD, HD)
        v_cols = pl.ds((len(KV_HEADS[g]) + at) * HD, HD)
        half = GROUP // 2

        def heads(i, carry):
            column = pl.multiple_of(p * WIDE + i * half * HD, HD)
            rows = jnp.concatenate(
                [q_ref[:, pl.ds(pl.multiple_of(column + g * HD, HD), HD)] for g in range(half)], axis=0)
            scores = lax.dot_general(
                rows, kv[:, k_cols], (((1,), (1,)), ((), ())),
                preferred_element_type=jnp.float32) * (1.0 / math.sqrt(HD))
            scores = scores.reshape(half, TOK, TOKENS) + bias[...][None]
            weights = jnp.exp(scores - jnp.max(scores, axis=-1, keepdims=True))
            total = jnp.sum(weights, axis=-1, keepdims=True)
            summed = jnp.dot(
                weights.reshape(half * TOK, TOKENS).astype(jnp.bfloat16), kv[:, v_cols],
                preferred_element_type=jnp.float32)
            done = (summed.reshape(half, TOK, HD) / total).astype(jnp.bfloat16)
            for g in range(half):
                att[at_rows(z, w), pl.ds(pl.multiple_of(column + g * HD, HD), HD)] = done[g]
            return carry

        lax.fori_loop(0, 2, heads, 0)
        ref = piece(p, z, w)
        n1, n2 = planes[ROUTES[p]]
        if ROUTES[p] == "l":
            send(ref, l_sems.at[0], z * 4 + n1)
            send(ref, l_sems.at[1], z * 4 + n2)
            out_along_z(p, ref, l_sem(p, z, 0))
        else:
            out_along_z(p, ref, z_sem(p, z, 0))
            send(ref, p_sems.at[p, 0], z * 4 + n1)
            send(ref, p_sems.at[p, 4], z * 4 + n2)

    def from_z(p, t):
        n1, n2 = planes[ROUTES[p]]
        ref = piece(p, layers[t], w)
        sem = z_sem(p, layers[t], 0)
        arrive(ref, sem)
        on_along_z(ref, sem, layers[t])
        send(ref, p_sems.at[p, t], z * 4 + n1)
        send(ref, p_sems.at[p, 4 + t], z * 4 + n2)

    def from_n1(p, t):
        n1, n2 = planes[ROUTES[p]]
        ref = piece(p, layers[t], n1)
        arrive(ref, p_sems.at[p, t])
        send(ref, p_sems.at[p, 8 + t], z * 4 + n2)

    def from_n2(p, c):
        n1, n2 = planes[ROUTES[p]]
        for t in range(NZ):
            arrive(piece(p, layers[t], w_d if c else n2), p_sems.at[p, 4 + 4 * c + t])

    def columns_of(p):
        n1, n2 = planes[ROUTES[p]]
        return (w, n1, n2, w_d)

    def l_from_n1(p):
        n1, n2 = planes[ROUTES[p]]
        ref = piece(p, z, n1)
        arrive(ref, l_sems.at[0])
        send(ref, l_sems.at[2], z * 4 + n2)
        out_along_z(p, ref, l_sem(p, z, 1))

    def l_from_n2(p, c):
        ref = piece(p, z, columns_of(p)[2 + c])
        arrive(ref, l_sems.at[1 + c])
        out_along_z(p, ref, l_sem(p, z, 2 + c))

    def l_from_z(p, t, c):
        ref = piece(p, layers[t], columns_of(p)[c])
        sem = l_sem(p, layers[t], c)
        arrive(ref, sem)
        on_along_z(ref, sem, layers[t])

    waited = []

    def project(p, rows):
        if not waited:
            waited.append(True)
            pltpu.make_async_copy(w_hbm, wt, w_sem).wait()
        left = jnp.concatenate([att[r, pl.ds(p * WIDE, WIDE)] for r in rows], axis=0)

        def tile(n, carry):
            cols = pl.ds(pl.multiple_of(n * 256, 256), 256)
            part = jnp.dot(left, wt[pl.ds(p * WIDE, WIDE), cols], preferred_element_type=jnp.float32)
            for i, r in enumerate(rows):
                acc[r, cols] += part[i * TOK:(i + 1) * TOK]
            return carry

        lax.fori_loop(0, acc.shape[1] // 256, tile, 0)

    def project_column(p, c):
        project(p, [at_rows(layer, columns_of(p)[c]) for layer in range(NZ)])

    def project_layer(p, t):
        project(p, [at_rows(layers[t], c) for c in range(4)])

    pltpu.make_async_copy(w_hbm, wt, w_sem).start()
    own = at_rows(z, w)
    for g, heads in enumerate(KV_HEADS):
        kvs[g][...] = jnp.zeros_like(kvs[g])
        for i, p in enumerate(heads):
            kvs[g][own, pl.ds(i * HD, HD)] = k_ref[:, pl.ds(p * HD, HD)]
            kvs[g][own, pl.ds((len(heads) + i) * HD, HD)] = v_ref[:, pl.ds(p * HD, HD)]
    square = (TOK, TOK)
    diagonal = lax.broadcasted_iota(jnp.int32, square, 0) == lax.broadcasted_iota(jnp.int32, square, 1)
    along = jnp.broadcast_to(seg_ref[...].astype(jnp.float32), square)
    down = jnp.sum(jnp.where(diagonal, along, 0.0), axis=1, keepdims=True)
    kv0[own, pl.ds(2 * HD, HD)] = jnp.broadcast_to(down, (TOK, HD)).astype(jnp.bfloat16)

    barrier = pltpu.get_barrier_semaphore()

    def greet(device, at_core):
        pl.semaphore_signal(barrier, inc=1, device_id=(device, at_core), device_id_type=MESH)

    greet(me, 1 - core)
    greet(z * 4 + w_x, core)
    greet(z * 4 + w_y, core)
    pl.when(has_up)(lambda: greet(me + 4, core))
    pl.when(has_down)(lambda: greet(me - 4, core))
    acc[...] = jnp.zeros_like(acc)
    inner = jnp.logical_and(has_up, has_down)
    pl.semaphore_wait(barrier, jnp.where(inner, 5, 4))

    steps = {"kv": kv_own, "kvz": kv_z, "kvn1": kv_n1, "kvn2": kv_n2, "mask": make_mask,
             "attn": attend, "z": from_z, "n1": from_n1, "n2": from_n2,
             "l1": l_from_n1, "l2": l_from_n2, "lz": l_from_z,
             "mm": project_column, "ml": project_layer}

    final = final_steps()
    mirror = {"own": "own", "A": "B", "B": "A", "D": "D"}
    places = {"own": w, "A": w_a, "B": w_b, "D": w_d}
    shares = []

    def share_of(t, c):
        rows = at_rows(layers[t], places[c])
        sem = tp_sems.at[layers[t] * 4 + places[c]]
        copy = pltpu.make_async_remote_copy(
            src_ref=outgoing.at[rows], dst_ref=incoming.at[rows],
            send_sem=share_sems.at[4 * t + list(places).index(c)], recv_sem=sem,
            device_id=(me, 1 - core), device_id_type=MESH)
        return rows, copy, layers[t] // 2 == core

    def hand_over(t, c):
        rows, copy, ours = share_of(t, c)

        def start():
            outgoing[rows, :] = acc[rows, :].astype(jnp.bfloat16)
            copy.start()

        pl.when(jnp.logical_not(ours))(start)
        shares.append((copy, ours))

    def put_out(t, c):
        rows, copy, ours = share_of(t, c)

        def finish():
            copy.wait_recv()
            total = acc[rows, :] + incoming[rows, :].astype(jnp.float32)
            at = pl.multiple_of((layers[t] - 2 * core) * LAYER + places[c] * TOK, TOK)
            out_ref[pl.ds(at, TOK), :] = total.astype(jnp.bfloat16)

        pl.when(ours)(finish)

    blocks = sorted(final, key=lambda b: max(final[b], final[b[0], mirror[b[1]]]))
    early = max(i for i, step in enumerate(ORDER) if step[0] not in ("mm", "ml"))
    for i, step in enumerate(ORDER):
        if i == early:
            while blocks and max(final[blocks[0]], final[blocks[0][0], mirror[blocks[0][1]]]) < i:
                put_out(*blocks.pop(0))
        steps[step[0]](*step[1:])
        for block in final:
            if final[block] == i:
                hand_over(*block)
    for block in blocks:
        put_out(*block)
    for copy, ours in shares:
        pl.when(jnp.logical_not(ours))(copy.wait_send)
    for copy, guard in sends:
        if guard is None:
            copy.wait_send()
        else:
            pl.when(guard)(copy.wait_send)


def final_steps():
    final = {}
    for i, step in enumerate(ORDER):
        if step[0] == "mm":
            route = ROUTES[step[1]]
            column = ("own", "B" if route == "b" else "A", "A" if route == "b" else "B", "D")[step[2]]
            final.update({(t, column): i for t in range(NZ)})
        elif step[0] == "ml":
            final.update({(step[2], column): i for column in ("own", "A", "B", "D")})
    return final


def count_sends():
    each = {"kv": 3, "kvz": 3, "kvn1": 1, "z": 3, "n1": 1, "l1": 3, "l2": 2, "lz": 1, "attn": 4}
    return sum(each.get(step[0], 0) for step in ORDER)


def kernel_body(queries, keys, values, segment_ids, out_weight):
    segments = segment_ids.reshape(1, TOK)
    width = out_weight.shape[1]
    vmem = pl.BlockSpec(memory_space=pltpu.VMEM)
    dma = pltpu.SemaphoreType.DMA
    return pl.pallas_call(
        block_kernel,
        out_shape=jax.ShapeDtypeStruct((TOKENS // 2, width), jnp.bfloat16),
        in_specs=[vmem, vmem, vmem, vmem, pl.BlockSpec(memory_space=pl.ANY)],
        out_specs=vmem,
        scratch_shapes=[
            *(pltpu.VMEM((TOKENS, cols), jnp.bfloat16) for cols in KV_COLS),
            pltpu.VMEM((TOKENS, HEADS * WIDE), jnp.bfloat16),
            pltpu.VMEM((HEADS * WIDE, width), jnp.bfloat16),
            pltpu.VMEM((TOKENS, width), jnp.float32),
            pltpu.VMEM((TOK, TOKENS), jnp.float32),
            pltpu.VMEM((TOKENS, width), jnp.bfloat16),
            pltpu.VMEM((TOKENS, width), jnp.bfloat16),
            dma,
            dma((count_sends(),)),
            dma((KV_GROUPS, 16)),
            dma((HEADS, NZ)),
            dma((HEADS, 12)),
            dma((20,)),
            dma((16,)),
            dma((16,)),
        ],
        compiler_params=pltpu.CompilerParams(
            collective_id=0, has_side_effects=True, vmem_limit_bytes=56 * 1024 * 1024),
        cost_estimate=pl.CostEstimate(
            flops=2 * TOKENS * HEADS * WIDE * width, bytes_accessed=16 * 2**20, transcendentals=2**21),
    )(queries, keys, values, segments, out_weight)


def solution(mesh):
    fits = mesh.shape["seq"] == 4 * NZ and mesh.shape["tp"] == 2
    return jax.shard_map(
        kernel_body if fits else body,
        mesh=mesh,
        in_specs=(P("seq", "tp"), P("seq", "tp"), P("seq", "tp"), P("seq"), P("tp", "seq")),
        out_specs=P("tp", "seq"),
        check_vma=False,
    )
```

```python
import functools
import math

import jax
import jax.numpy as jnp
from jax import lax
from jax.experimental import pallas as pl
from jax.experimental.pallas import tpu as pltpu
from jax.sharding import PartitionSpec as P

HD = 128
GROUP = 8
MESH = pl.DeviceIdType.MESH

masked_score = -1e30


def body(queries, keys, values, segment_ids, out_weight):
    seq_rank = lax.axis_index("seq")
    tok_count = queries.shape[0]
    local_heads = keys.shape[1] // HD
    score_scale = 1.0 / math.sqrt(HD)
    all_segments = lax.all_gather(segment_ids, "seq", axis=0, tiled=True)
    offsets = jnp.arange(tok_count, dtype=jnp.int32)
    positions = seq_rank * tok_count + offsets
    query_segments = jnp.take(all_segments, positions)
    grouped = queries.reshape(tok_count, local_heads, GROUP, HD)
    key_block = lax.all_gather(keys, "seq", axis=0, tiled=True)
    value_block = lax.all_gather(values, "seq", axis=0, tiled=True)
    block_rows = key_block.shape[0]
    key_pos = jnp.arange(block_rows, dtype=jnp.int32)
    allowed = (key_pos[None, :] <= positions[:, None]) & (
        all_segments[None, :] == query_segments[:, None]
    )
    running_max = jnp.full((local_heads, tok_count, GROUP), masked_score, jnp.float32)
    key_heads = key_block.reshape(block_rows, local_heads, HD)
    value_heads = value_block.reshape(block_rows, local_heads, HD)
    scores = (
        jnp.einsum("thgd,nhd->htgn", grouped, key_heads, preferred_element_type=jnp.float32)
        * score_scale
    )
    keep_mask = allowed[None, :, None, :]
    new_max = jnp.maximum(running_max, jnp.max(jnp.where(keep_mask, scores, masked_score), axis=-1))
    weights = jnp.where(keep_mask, jnp.exp(scores - new_max[..., None]), 0.0)
    running_sum = jnp.sum(weights, axis=-1)
    summed = jnp.einsum(
        "htgn,nhd->htgd",
        weights.astype(jnp.bfloat16),
        value_heads,
        preferred_element_type=jnp.float32,
    )
    attended = (
        (summed / running_sum[..., None])
        .transpose(1, 0, 2, 3)
        .reshape(tok_count, local_heads * GROUP * HD)
    )
    attended = attended.astype(jnp.bfloat16)
    partial_out = jnp.dot(
        lax.all_gather(attended, "seq", axis=0, tiled=True),
        out_weight,
        preferred_element_type=jnp.float32,
    )
    summed_out = lax.psum_scatter(
        partial_out.astype(jnp.bfloat16), "tp", scatter_dimension=0, tiled=True
    )
    return summed_out


NZ = 4
TOK = 64
LAYER = 4 * TOK
TOKENS = NZ * LAYER
HEADS = 4
WIDE = GROUP * HD

ROUTES = ("l", "a", "b", "a")
KV_HEADS = ((0,), (1, 2), (3,))
KV_COLS = tuple(2 * len(heads) * HD + (HD if g == 0 else 0) for g, heads in enumerate(KV_HEADS))
KV_GROUPS = len(KV_HEADS)
KV_REACH = 9

ORDER = (
    ("kv", 0), ("kv", 1), ("kvz", 0, 1), ("kvn1", 0, 0), ("kvz", 1, 1), ("kvz", 0, 2), ("kvz", 0, 3),
    ("kvn1", 0, 1), ("kv", 2), ("kvn1", 0, 2), ("kvz", 1, 2), ("kvz", 1, 3), ("kvn1", 1, 1), ("kvn2", 0, 0),
    ("kvz", 2, 1), ("kvn1", 1, 0), ("kvn1", 1, 3), ("kvn2", 1, 3), ("kvz", 2, 2), ("kvn2", 0, 1),
    ("kvn1", 0, 3), ("kvn2", 0, 2), ("kvn2", 0, 3), ("mask",), ("kvn1", 1, 2), ("attn", 0), ("kvn2", 1, 1),
    ("kvn2", 1, 2), ("kvn1", 2, 0), ("kvn2", 1, 0), ("kvn1", 2, 2), ("kvz", 2, 3), ("l1", 0), ("kvn1", 2, 3),
    ("attn", 2), ("l2", 0, 1), ("attn", 1), ("z", 2, 1), ("kvn2", 2, 0), ("n1", 1, 0), ("kvn1", 2, 1),
    ("kvn2", 2, 2), ("lz", 0, 1, 3), ("l2", 0, 0), ("z", 1, 1), ("z", 2, 2), ("n1", 2, 0), ("lz", 0, 2, 3),
    ("n1", 2, 1), ("kvn2", 2, 3), ("lz", 0, 1, 1), ("n1", 1, 1), ("z", 1, 2), ("kvn2", 2, 1), ("attn", 3),
    ("z", 1, 3), ("z", 2, 3), ("lz", 0, 1, 2), ("lz", 0, 2, 2), ("n1", 1, 2), ("z", 3, 1), ("lz", 0, 1, 0),
    ("z", 3, 2), ("mm", 1, 0), ("n2", 1, 0), ("z", 3, 3), ("mm", 2, 0), ("ml", 0, 0), ("n1", 2, 3),
    ("n1", 2, 2), ("lz", 0, 2, 1), ("n1", 1, 3), ("mm", 1, 1), ("n1", 3, 1), ("mm", 1, 2), ("lz", 0, 3, 3),
    ("n2", 2, 0), ("ml", 0, 1), ("n1", 3, 0), ("n1", 3, 3), ("lz", 0, 2, 0), ("mm", 2, 1), ("n2", 3, 0),
    ("mm", 3, 2), ("lz", 0, 3, 1), ("ml", 0, 2), ("n1", 3, 2), ("mm", 2, 2), ("mm", 3, 1), ("n2", 2, 1),
    ("lz", 0, 3, 0), ("mm", 2, 3), ("n2", 1, 1), ("mm", 3, 0), ("mm", 1, 3), ("lz", 0, 3, 2), ("n2", 3, 1),
    ("mm", 3, 3), ("ml", 0, 3),)


def block_kernel(q_ref, k_ref, v_ref, seg_ref, w_hbm, out_ref,
                 kv0, kv1, kv2, att, wt, acc, bias, outgoing, incoming,
                 w_sem, send_sems, kv_sems, z_sems, p_sems, l_sems, share_sems, tp_sems):
    me = lax.axis_index("seq")
    core = lax.axis_index("tp")
    z = me // 4
    w = me % 4
    x = w % 2
    y = w // 2
    w_x = y * 2 + (1 - x)
    w_y = (1 - y) * 2 + x
    w_d = (1 - y) * 2 + (1 - x)
    w_a = jnp.where(core == 0, w_x, w_y)
    w_b = jnp.where(core == 0, w_y, w_x)
    planes = {"a": (w_a, w_b), "b": (w_b, w_a), "l": (w_a, w_b)}

    def nearest(t):
        table = ((0, 1, 2, 3), (1, 0, 2, 3), (2, 3, 1, 0), (3, 2, 1, 0))
        at = jnp.int32(table[0][t])
        for layer in range(1, NZ):
            at = jnp.where(z == layer, table[layer][t], at)
        return at

    layers = [z if t == 0 else nearest(t) for t in range(NZ)]
    has_up = z < NZ - 1
    has_down = z > 0
    sends = []

    def at_rows(layer, column):
        return pl.ds(pl.multiple_of(layer * LAYER + column * TOK, TOK), TOK)

    def copy_of(ref, recv_sem, device, send_sem):
        return pltpu.make_async_remote_copy(
            src_ref=ref, dst_ref=ref, send_sem=send_sem, recv_sem=recv_sem,
            device_id=(device, core), device_id_type=MESH)

    def send(ref, recv_sem, device, guard=None):
        copy = copy_of(ref, recv_sem, device, send_sems.at[len(sends)])
        sends.append((copy, guard))
        if guard is None:
            copy.start()
        else:
            pl.when(guard)(copy.start)

    def arrive(ref, recv_sem, guard=None):
        copy = copy_of(ref, recv_sem, me, send_sems.at[0])
        if guard is None:
            copy.wait_recv()
        else:
            pl.when(guard)(copy.wait_recv)

    kvs = (kv0, kv1, kv2)

    last = NZ - 1

    def kv_route(g):
        return planes["a"] if g % 2 == 0 else planes["b"]

    def reads(column, source, t):
        blocks = 4 * t + column - source
        return (z >= t) & (blocks >= 1) & (blocks <= KV_REACH)

    def rises(t):
        return 4 * t - w <= KV_REACH

    def kv_own(g):
        kv_out(g, 0)

    def kv_out(g, t):
        n1, n2 = kv_route(g)
        ref = kvs[g].at[at_rows(z - t, w)]
        if t < last:
            send(ref, kv_sems.at[g, t + 1], me + 4, has_up & (z >= t) & rises(t + 1))
        send(ref, kv_sems.at[g, 4 + t], z * 4 + n1, reads(n1, w, t) | reads(w_d, w, t))
        send(ref, kv_sems.at[g, 8 + t], z * 4 + n2, reads(n2, w, t))

    def kv_z(g, t):
        arrive(kvs[g].at[at_rows(z - t, w)], kv_sems.at[g, t], (z >= t) & rises(t))
        kv_out(g, t)

    def kv_n1(g, t):
        n1, n2 = kv_route(g)
        ref = kvs[g].at[at_rows(z - t, n1)]
        arrive(ref, kv_sems.at[g, 4 + t], reads(w, n1, t) | reads(n2, n1, t))
        send(ref, kv_sems.at[g, 12 + t], z * 4 + n2, reads(n2, n1, t))

    def kv_n2(g, t):
        n1, n2 = kv_route(g)
        arrive(kvs[g].at[at_rows(z - t, n2)], kv_sems.at[g, 8 + t], reads(w, n2, t))
        arrive(kvs[g].at[at_rows(z - t, w_d)], kv_sems.at[g, 12 + t], reads(w, w_d, t))

    def make_mask():
        ones = jnp.full((8, HD), 1.0 / HD, jnp.bfloat16)
        key_segments = lax.dot_general(
            ones, kv0[:, 2 * HD:3 * HD], (((1,), (1,)), ((), ())),
            preferred_element_type=jnp.float32)[0:1, :]
        query_segments = kv0[at_rows(z, w), pl.ds(2 * HD, HD)][:, 0:1].astype(jnp.float32)
        key_at = lax.broadcasted_iota(jnp.int32, (TOK, TOKENS), 1)
        query_at = me * TOK + lax.broadcasted_iota(jnp.int32, (TOK, TOKENS), 0)
        allowed = (key_at <= query_at) & (key_segments == query_segments)
        bias[...] = jnp.where(allowed, 0.0, masked_score)

    def piece(p, layer, column):
        return att.at[at_rows(layer, column), pl.ds(p * WIDE, WIDE)]

    def z_sem(p, layer, column):
        return z_sems.at[p, layer]

    def l_sem(p, layer, c):
        return l_sems.at[4 + c * 4 + layer]

    def out_along_z(p, ref, sem):
        send(ref, sem, me + 4, has_up)
        send(ref, sem, me - 4, has_down)

    def on_along_z(ref, sem, layer):
        upward = layer < z
        further = jnp.where(upward, has_up, has_down)
        send(ref, sem, jnp.where(upward, me + 4, me - 4), further)

    def attend(p):
        g = next(i for i, heads in enumerate(KV_HEADS) if p in heads)
        kv, at = kvs[g], KV_HEADS[g].index(p)
        k_cols = pl.ds(at * HD, HD)
        v_cols = pl.ds((len(KV_HEADS[g]) + at) * HD, HD)
        half = GROUP // 2

        def heads(i, carry):
            column = pl.multiple_of(p * WIDE + i * half * HD, HD)
            rows = jnp.concatenate(
                [q_ref[:, pl.ds(pl.multiple_of(column + g * HD, HD), HD)] for g in range(half)], axis=0)
            scores = lax.dot_general(
                rows, kv[:, k_cols], (((1,), (1,)), ((), ())),
                preferred_element_type=jnp.float32) * (1.0 / math.sqrt(HD))
            scores = scores.reshape(half, TOK, TOKENS) + bias[...][None]
            weights = jnp.exp(scores - jnp.max(scores, axis=-1, keepdims=True))
            total = jnp.sum(weights, axis=-1, keepdims=True)
            summed = jnp.dot(
                weights.reshape(half * TOK, TOKENS).astype(jnp.bfloat16), kv[:, v_cols],
                preferred_element_type=jnp.float32)
            done = (summed.reshape(half, TOK, HD) / total).astype(jnp.bfloat16)
            for g in range(half):
                att[at_rows(z, w), pl.ds(pl.multiple_of(column + g * HD, HD), HD)] = done[g]
            return carry

        lax.fori_loop(0, 2, heads, 0)
        ref = piece(p, z, w)
        n1, n2 = planes[ROUTES[p]]
        if ROUTES[p] == "l":
            send(ref, l_sems.at[0], z * 4 + n1)
            send(ref, l_sems.at[1], z * 4 + n2)
            out_along_z(p, ref, l_sem(p, z, 0))
        else:
            out_along_z(p, ref, z_sem(p, z, 0))
            send(ref, p_sems.at[p, 0], z * 4 + n1)
            send(ref, p_sems.at[p, 4], z * 4 + n2)

    def from_z(p, t):
        n1, n2 = planes[ROUTES[p]]
        ref = piece(p, layers[t], w)
        sem = z_sem(p, layers[t], 0)
        arrive(ref, sem)
        on_along_z(ref, sem, layers[t])
        send(ref, p_sems.at[p, t], z * 4 + n1)
        send(ref, p_sems.at[p, 4 + t], z * 4 + n2)

    def from_n1(p, t):
        n1, n2 = planes[ROUTES[p]]
        ref = piece(p, layers[t], n1)
        arrive(ref, p_sems.at[p, t])
        send(ref, p_sems.at[p, 8 + t], z * 4 + n2)

    def from_n2(p, c):
        n1, n2 = planes[ROUTES[p]]
        for t in range(NZ):
            arrive(piece(p, layers[t], w_d if c else n2), p_sems.at[p, 4 + 4 * c + t])

    def columns_of(p):
        n1, n2 = planes[ROUTES[p]]
        return (w, n1, n2, w_d)

    def l_from_n1(p):
        n1, n2 = planes[ROUTES[p]]
        ref = piece(p, z, n1)
        arrive(ref, l_sems.at[0])
        send(ref, l_sems.at[2], z * 4 + n2)
        out_along_z(p, ref, l_sem(p, z, 1))

    def l_from_n2(p, c):
        ref = piece(p, z, columns_of(p)[2 + c])
        arrive(ref, l_sems.at[1 + c])
        out_along_z(p, ref, l_sem(p, z, 2 + c))

    def l_from_z(p, t, c):
        ref = piece(p, layers[t], columns_of(p)[c])
        sem = l_sem(p, layers[t], c)
        arrive(ref, sem)
        on_along_z(ref, sem, layers[t])

    waited = []

    def project(p, rows):
        if not waited:
            waited.append(True)
            pltpu.make_async_copy(w_hbm, wt, w_sem).wait()
        left = jnp.concatenate([att[r, pl.ds(p * WIDE, WIDE)] for r in rows], axis=0)

        def tile(n, carry):
            cols = pl.ds(pl.multiple_of(n * 256, 256), 256)
            part = jnp.dot(left, wt[pl.ds(p * WIDE, WIDE), cols], preferred_element_type=jnp.float32)
            for i, r in enumerate(rows):
                acc[r, cols] += part[i * TOK:(i + 1) * TOK]
            return carry

        lax.fori_loop(0, acc.shape[1] // 256, tile, 0)

    def project_column(p, c):
        project(p, [at_rows(layer, columns_of(p)[c]) for layer in range(NZ)])

    def project_layer(p, t):
        project(p, [at_rows(layers[t], c) for c in range(4)])

    pltpu.make_async_copy(w_hbm, wt, w_sem).start()
    own = at_rows(z, w)
    for g, heads in enumerate(KV_HEADS):
        kvs[g][...] = jnp.zeros_like(kvs[g])
        for i, p in enumerate(heads):
            kvs[g][own, pl.ds(i * HD, HD)] = k_ref[:, pl.ds(p * HD, HD)]
            kvs[g][own, pl.ds((len(heads) + i) * HD, HD)] = v_ref[:, pl.ds(p * HD, HD)]
    square = (TOK, TOK)
    diagonal = lax.broadcasted_iota(jnp.int32, square, 0) == lax.broadcasted_iota(jnp.int32, square, 1)
    along = jnp.broadcast_to(seg_ref[...].astype(jnp.float32), square)
    down = jnp.sum(jnp.where(diagonal, along, 0.0), axis=1, keepdims=True)
    kv0[own, pl.ds(2 * HD, HD)] = jnp.broadcast_to(down, (TOK, HD)).astype(jnp.bfloat16)

    barrier = pltpu.get_barrier_semaphore()

    def greet(device, at_core):
        pl.semaphore_signal(barrier, inc=1, device_id=(device, at_core), device_id_type=MESH)

    greet(me, 1 - core)
    greet(z * 4 + w_x, core)
    greet(z * 4 + w_y, core)
    pl.when(has_up)(lambda: greet(me + 4, core))
    pl.when(has_down)(lambda: greet(me - 4, core))
    acc[...] = jnp.zeros_like(acc)
    inner = jnp.logical_and(has_up, has_down)
    pl.semaphore_wait(barrier, jnp.where(inner, 5, 4))

    steps = {"kv": kv_own, "kvz": kv_z, "kvn1": kv_n1, "kvn2": kv_n2, "mask": make_mask,
             "attn": attend, "z": from_z, "n1": from_n1, "n2": from_n2,
             "l1": l_from_n1, "l2": l_from_n2, "lz": l_from_z,
             "mm": project_column, "ml": project_layer}

    final = final_steps()
    mirror = {"own": "own", "A": "B", "B": "A", "D": "D"}
    places = {"own": w, "A": w_a, "B": w_b, "D": w_d}
    shares = []

    def share_of(t, c):
        rows = at_rows(layers[t], places[c])
        sem = tp_sems.at[layers[t] * 4 + places[c]]
        copy = pltpu.make_async_remote_copy(
            src_ref=outgoing.at[rows], dst_ref=incoming.at[rows],
            send_sem=share_sems.at[4 * t + list(places).index(c)], recv_sem=sem,
            device_id=(me, 1 - core), device_id_type=MESH)
        return rows, copy, layers[t] // 2 == core

    def hand_over(t, c):
        rows, copy, ours = share_of(t, c)

        def start():
            outgoing[rows, :] = acc[rows, :].astype(jnp.bfloat16)
            copy.start()

        pl.when(jnp.logical_not(ours))(start)
        shares.append((copy, ours))

    def put_out(t, c):
        rows, copy, ours = share_of(t, c)

        def finish():
            copy.wait_recv()
            total = acc[rows, :] + incoming[rows, :].astype(jnp.float32)
            at = pl.multiple_of((layers[t] - 2 * core) * LAYER + places[c] * TOK, TOK)
            out_ref[pl.ds(at, TOK), :] = total.astype(jnp.bfloat16)

        pl.when(ours)(finish)

    blocks = sorted(final, key=lambda b: max(final[b], final[b[0], mirror[b[1]]]))
    early = max(i for i, step in enumerate(ORDER) if step[0] not in ("mm", "ml"))
    for i, step in enumerate(ORDER):
        if i == early:
            while blocks and max(final[blocks[0]], final[blocks[0][0], mirror[blocks[0][1]]]) < i:
                put_out(*blocks.pop(0))
        steps[step[0]](*step[1:])
        for block in final:
            if final[block] == i:
                hand_over(*block)
    for block in blocks:
        put_out(*block)
    for copy, ours in shares:
        pl.when(jnp.logical_not(ours))(copy.wait_send)
    for copy, guard in sends:
        if guard is None:
            copy.wait_send()
        else:
            pl.when(guard)(copy.wait_send)


def final_steps():
    final = {}
    for i, step in enumerate(ORDER):
        if step[0] == "mm":
            route = ROUTES[step[1]]
            column = ("own", "B" if route == "b" else "A", "A" if route == "b" else "B", "D")[step[2]]
            final.update({(t, column): i for t in range(NZ)})
        elif step[0] == "ml":
            final.update({(step[2], column): i for column in ("own", "A", "B", "D")})
    return final


def count_sends():
    each = {"kv": 3, "kvz": 3, "kvn1": 1, "z": 3, "n1": 1, "l1": 3, "l2": 2, "lz": 1, "attn": 4}
    return sum(each.get(step[0], 0) for step in ORDER)


def kernel_body(queries, keys, values, segment_ids, out_weight):
    segments = segment_ids.reshape(1, TOK)
    width = out_weight.shape[1]
    vmem = pl.BlockSpec(memory_space=pltpu.VMEM)
    dma = pltpu.SemaphoreType.DMA
    return pl.pallas_call(
        block_kernel,
        out_shape=jax.ShapeDtypeStruct((TOKENS // 2, width), jnp.bfloat16),
        in_specs=[vmem, vmem, vmem, vmem, pl.BlockSpec(memory_space=pl.ANY)],
        out_specs=vmem,
        scratch_shapes=[
            *(pltpu.VMEM((TOKENS, cols), jnp.bfloat16) for cols in KV_COLS),
            pltpu.VMEM((TOKENS, HEADS * WIDE), jnp.bfloat16),
            pltpu.VMEM((HEADS * WIDE, width), jnp.bfloat16),
            pltpu.VMEM((TOKENS, width), jnp.float32),
            pltpu.VMEM((TOK, TOKENS), jnp.float32),
            pltpu.VMEM((TOKENS, width), jnp.bfloat16),
            pltpu.VMEM((TOKENS, width), jnp.bfloat16),
            dma,
            dma((count_sends(),)),
            dma((KV_GROUPS, 16)),
            dma((HEADS, NZ)),
            dma((HEADS, 12)),
            dma((20,)),
            dma((16,)),
            dma((16,)),
        ],
        compiler_params=pltpu.CompilerParams(
            collective_id=0, has_side_effects=True, vmem_limit_bytes=56 * 1024 * 1024),
        cost_estimate=pl.CostEstimate(
            flops=2 * TOKENS * HEADS * WIDE * width, bytes_accessed=16 * 2**20, transcendentals=2**21),
    )(queries, keys, values, segments, out_weight)


def solution(mesh):
    fits = mesh.shape["seq"] == 4 * NZ and mesh.shape["tp"] == 2
    return jax.shard_map(
        kernel_body if fits else body,
        mesh=mesh,
        in_specs=(P("seq", "tp"), P("seq", "tp"), P("seq", "tp"), P("seq"), P("tp", "seq")),
        out_specs=P("tp", "seq"),
        check_vma=False,
    )
```
